32 devices in a mesh: groups: 2 (over x), node: 16 (over z, y, core).
Axes of the slice: x: 2, y: 2, z: 4, core: 2. Of those that a mesh axis runs over, the one named last changes fastest.
Arguments:
- unit_costs: bfloat16 [1024, 24, 2048], P(('groups', 'node')), parts along dimension 0, may hold values from -15 to 15
- hour_duals: bfloat16 [1024, 24, 2048], P(('groups', 'node')), parts along dimension 0, may hold values from -3 to 3
- inverse: bfloat16 [2048, 2048], replicated, may hold values from -0.5 to 1.5, as said below
- weights: int32 [1024], P(('groups', 'node')), parts along dimension 0, may hold values from 1 to 120
- section_three: int32 [1024], P(('groups', 'node')), parts along dimension 0, may hold values from 0 to 63, as said below
- prev_first: bfloat16 [16, 2048], P('groups'), parts along dimension 0, may hold values from -6 to 6
- prev_second: bfloat16 [32, 8, 512], P(('groups', 'node')), parts along dimension 0, may hold values from -6 to 6
- prev_third: bfloat16 [128, 8, 2048], P(('groups', 'node')), parts along dimension 0, may hold values from -6 to 6
- eta_mean: float32 [2], P('groups'), parts along dimension 0, may hold values from -2 to -1
- eta_duals: float32 [1024], P(('groups', 'node')), parts along dimension 0, may hold values from -1.2 to 1.2
Outputs:
- duals_new: bfloat16 [1024, 24, 2048], P(('groups', 'node')), parts along dimension 0
- first_avg: float32 [16, 2048], P('groups'), parts along dimension 0
- second_avg: float32 [32, 8, 512], P(('groups', 'node')), parts along dimension 0
- third_avg: float32 [128, 8, 2048], P(('groups', 'node')), parts along dimension 0
- eta_avg: float32 [2], P('groups'), parts along dimension 0
- eta_duals_new: float32 [1024], P(('groups', 'node')), parts along dimension 0
The draws below stay inside these ranges and needn't reach their ends.
There are 2 independent parts, one for each index of `groups`. The reference program is written for one: setup_inputs(seed, part) draws one part's arguments, and reference() takes and returns one part's arrays. A program takes and returns all parts, laid end to end along the dimension named above; an argument that names none is the same for every part. Nothing has to cross between parts.
Inputs may be any that keep to these rules, and one draw needn't show every extreme that they name: `inverse`: A fixed matrix of order 2048. `section_three`: scenario s lies below section-2 node n = s // 128: its section-3 node is n * 16 + b with b from 0 to 15; every section-3 node holds exactly 8 scenarios.
All inputs are finite; a program needn't handle non-finite values.
Results may differ from the reference program's by a relative error of at most 0.0082.
Values may be sent and summed in bfloat16 or wider, within the bound.
A program may use at most 128 MiB of HBM per device.

```python
import math
import jax
import jax.numpy as jnp

GEN = 2048
HS = 8
BRANCH = 16
SC_DEV = 32
HOURS = 24
SCEN = 512
N2 = 4
N3 = 64


def draw_unit_costs(key, part):
    key_level, key_base, key_noise = jax.random.split(key, 3)
    node_level = jnp.exp(jax.random.uniform(key_level, (N2, 1, 1), jnp.float32, math.log(0.5), math.log(2.0)))
    scen_level = jnp.repeat(node_level, 4 * SC_DEV, axis=0)
    base_cost = 1.0 + 0.8 * jnp.clip(jax.random.normal(key_base, (1, HOURS, GEN), jnp.float32), -3.0, 3.0)
    noise = 0.7 * jnp.clip(jax.random.normal(key_noise, (SCEN, HOURS, GEN), jnp.float32), -3.0, 3.0)
    return (scen_level * (base_cost + noise)).astype(jnp.bfloat16)


def draw_inverse(key, part):
    key_diag, key_off = jax.random.split(key, 2)
    diag_vals = jnp.exp(jax.random.uniform(key_diag, (GEN,), jnp.float32, math.log(0.4), math.log(1.2)))
    raw_noise = jnp.clip(jax.random.normal(key_off, (GEN, GEN), jnp.float32), -6.0, 6.0)
    off_part = (raw_noise + raw_noise.T) * (0.18 / math.sqrt(2.0 * GEN))
    coupled = jnp.full((GEN, GEN), 0.25 / GEN, jnp.float32)
    return (off_part + coupled + jnp.diag(diag_vals)).astype(jnp.bfloat16)


def draw_weights(key, part):
    base_part = jax.random.randint(key, (SCEN,), 1, 41, dtype=jnp.int32)
    rise_part = jnp.arange(SCEN, dtype=jnp.int32) * 80 // SCEN
    return (base_part + rise_part).astype(jnp.int32)


def draw_section_three(key, part):
    key_list = jax.random.split(key, N2)
    shuffles = jax.vmap(lambda one_key: jax.random.permutation(one_key, 4 * SC_DEV))(key_list)
    node_base = jnp.arange(N2, dtype=jnp.int32)[:, None] * BRANCH
    return (node_base + shuffles.astype(jnp.int32) % BRANCH).reshape(SCEN).astype(jnp.int32)


def block_levels(own_key, extent, cuts, smallest, high):
    def one(dim, parts):
        steps = jax.random.uniform(jax.random.fold_in(jax.random.fold_in(own_key, 6), dim), (parts,), jnp.float32, smallest / len(cuts), high / len(cuts))
        return jnp.repeat(jnp.exp(steps), extent[dim] // parts).reshape((-1,) + (1,) * (len(extent) - dim - 1))

    gain = one(*cuts[0])
    for cut in cuts[1:]:
        gain = gain * one(*cut)
    return gain


def normal_values(stream_key, dims, scale, most, cuts=(), kind=jnp.bfloat16):
    level = block_levels(stream_key, dims, cuts, -0.22, 0.18) if cuts else 1.0
    values = jax.random.normal(stream_key, dims, jnp.float32) * scale * level
    return jnp.minimum(jnp.maximum(values, -most), most).astype(kind)


def setup_inputs(seed: int = 0, part: int = 0) -> dict:
    keys = jax.random.split(jax.random.key(seed), 11)
    part_splits = jax.random.split(jax.random.fold_in(keys[10], part), 11)
    unit_costs = draw_unit_costs(jax.random.fold_in(jax.random.fold_in(keys[10], part), 71), part)
    hour_duals = normal_values(part_splits[1], (SCEN, HOURS, GEN), 0.5, 3.0, ((0, 16),))
    inverse = draw_inverse(jax.random.fold_in(keys[10], 71), part)
    weights = draw_weights(jax.random.fold_in(jax.random.fold_in(keys[10], part), 71), part)
    section_three = draw_section_three(jax.random.fold_in(jax.random.fold_in(keys[10], part), 71), part)
    prev_first = normal_values(part_splits[5], (HS, GEN), 1.0, 6.0)
    prev_second = normal_values(part_splits[6], (4 * N2, HS, GEN // 4), 1.0, 6.0, ((0, 16),))
    prev_third = normal_values(part_splits[7], (N3, HS, GEN), 1.0, 6.0, ((0, 16),))
    eta_mean = jnp.clip(jax.random.uniform(part_splits[8], (1,), jnp.float32, -2.0, -1.0), -2.0, -1.0)
    eta_duals = normal_values(part_splits[9], (SCEN,), 0.3, 1.2, ((0, 16),), jnp.float32)
    return dict(unit_costs=unit_costs, hour_duals=hour_duals, inverse=inverse, weights=weights, section_three=section_three, prev_first=prev_first, prev_second=prev_second, prev_third=prev_third, eta_mean=eta_mean, eta_duals=eta_duals)


PENALTY = 1.0
CVAR_WEIGHT = 0.25
CVAR_LEVEL = 0.75


def reference(unit_costs, hour_duals, inverse, weights, section_three, prev_first, prev_second, prev_third, eta_mean, eta_duals):
    scenarios = unit_costs.shape[0]
    block_len = 4 * SC_DEV
    section_two = jnp.arange(scenarios, dtype=jnp.int32) // block_len
    second_table = prev_second.reshape(N2, 4, HS, GEN // 4).transpose(0, 2, 1, 3).reshape(N2, HS, GEN)
    anchor = jnp.concatenate((
        jnp.broadcast_to(prev_first.astype(jnp.float32)[None], (scenarios, HS, GEN)),
        second_table.astype(jnp.float32)[section_two],
        prev_third.astype(jnp.float32)[section_three]), axis=1)
    target = (PENALTY * anchor - unit_costs.astype(jnp.float32) - hour_duals.astype(jnp.float32)).astype(jnp.bfloat16)
    solution = jnp.dot(target.reshape(scenarios * HOURS, GEN), inverse, preferred_element_type=jnp.float32).reshape(scenarios, HOURS, GEN)
    mass_vec = weights.astype(jnp.float32)
    mass_sum = jnp.sum(mass_vec)
    weighted = mass_vec[:, None, None] * solution
    first_avg = jnp.sum(weighted[:, :HS], axis=0) / mass_sum
    second_mass = jnp.sum(mass_vec.reshape(N2, block_len), axis=1)
    second_full = jnp.sum(weighted[:, HS:2 * HS].reshape(N2, block_len, HS, GEN), axis=1) / second_mass[:, None, None]
    third_mass = jax.ops.segment_sum(mass_vec, section_three, num_segments=N3)
    third_avg = jax.ops.segment_sum(weighted[:, 2 * HS:], section_three, num_segments=N3) / third_mass[:, None, None]
    new_anchor = jnp.concatenate((
        jnp.broadcast_to(first_avg[None], (scenarios, HS, GEN)),
        second_full[section_two],
        third_avg[section_three]), axis=1)
    duals_new = (hour_duals.astype(jnp.float32) + PENALTY * (solution - new_anchor)).astype(jnp.bfloat16)
    scen_cost = jnp.sum(unit_costs.astype(jnp.float32) * solution, axis=(1, 2)) / (HOURS * GEN)
    low_end = eta_mean[0] - (CVAR_WEIGHT + eta_duals) / PENALTY
    high_end = low_end + CVAR_WEIGHT / ((1.0 - CVAR_LEVEL) * PENALTY)
    eta_value = jnp.minimum(jnp.maximum(scen_cost, low_end), high_end)
    eta_level = jnp.sum(mass_vec * eta_value) / mass_sum
    eta_duals_new = eta_duals + PENALTY * (eta_value - eta_level)
    second_avg = second_full.reshape(N2, HS, 4, GEN // 4).transpose(0, 2, 1, 3).reshape(4 * N2, HS, GEN // 4)
    return (duals_new, first_avg, second_avg, third_avg, jnp.reshape(eta_level, (1,)), eta_duals_new)
```

```python
import functools

import jax
import jax.numpy as jnp
from jax import lax
from jax.experimental import pallas as pl
from jax.experimental.pallas import tpu as pltpu
from jax.sharding import PartitionSpec as P

BRANCH = 16
PENALTY = 1.0
CVAR_WEIGHT = 0.25
CVAR_LEVEL = 0.75
CHUNKS = 4
MESH = pl.DeviceIdType.MESH
F32 = jnp.float32
BF16 = jnp.bfloat16


def kernel(
    n,
    c_hbm,
    d_hbm,
    inv_hbm,
    w_ref,
    b_ref,
    b_smem,
    pf_ref,
    ps_ref,
    pt_hbm,
    em_ref,
    ed_ref,
    duals_ref,
    first_ref,
    second_ref,
    third_ref,
    level_ref,
    ednew_ref,
    c_ref,
    d_ref,
    inv_ref,
    t_ref,
    x_ref,
    s_ref,
    w_mat,
    tab_ref,
    avg_ref,
    tl_ref,
    pt_tab,
    sec_tab,
    meta_ref,
    eta_ref,
    x1_send,
    x1_recv,
    x2_send,
    x2_recv,
    fs_send,
    fs_recv,
    z_ref,
    cost_ref,
    load_sem,
    meta_ssem,
    meta_rsem,
    eta_ssem,
    eta_rsem,
    pt_ssem,
    pt_rsem,
    sec_ssem,
    sec_rsem,
    x1_ssem,
    x1_rsem,
    x2_ssem,
    x2_rsem,
    x3_ssem,
    x3_rsem,
    fs_ssem,
    fs_rsem,
    z_ssem,
    z_rsem,
    ag_ssem,
    ag_rsem,
):
    rows, cols = c_ref.shape
    scen = b_smem.shape[0]
    hours = rows // scen
    hs = hours // 3
    groups2 = n // 4
    width = cols // CHUNKS
    quart = cols // 4
    tile = min(256, width)
    half = BRANCH * hs // 2
    me = lax.axis_index("node")
    quarter = lax.rem(me, 4)
    core = lax.rem(me, 2)
    base = me - quarter
    team = lax.div(me, 4)
    core_peer = me + 1 - 2 * core
    far_peer = me + 2 - 4 * lax.rem(lax.div(me, 2), 2)
    far_q = lax.rem(quarter + 2, 4)
    core_q = quarter + 1 - 2 * core
    diag_q = lax.rem(core_q + 2, 4)

    def remote(src, dst, ssem, rsem, device):
        return pltpu.make_async_remote_copy(
            src_ref=src,
            dst_ref=dst,
            send_sem=ssem,
            recv_sem=rsem,
            device_id={"node": device},
            device_id_type=MESH,
        )

    def chunk(k):
        return pl.ds(k * width, width)

    def load(k, which):
        src, dst = ((c_hbm, c_ref), (d_hbm, d_ref), (inv_hbm, inv_ref))[which]
        return pltpu.make_async_copy(
            src.at[:, chunk(k)], dst.at[:, chunk(k)], load_sem.at[which, k]
        )

    for k in range(CHUNKS):
        load(k, 0).start()
        load(k, 1).start()
    for k in range(CHUNKS):
        load(k, 2).start()
    own_third = pltpu.make_async_copy(pt_hbm, pt_tab.at[quarter], load_sem.at[3, 0])
    own_third.start()

    barrier = pltpu.get_barrier_semaphore()

    @pl.loop(1, n)
    def _(r):
        pl.semaphore_signal(
            barrier, inc=1, device_id={"node": lax.rem(me + r, n)}, device_id_type=MESH
        )

    weight_row = w_ref[...].astype(F32)
    branch_row = lax.rem(b_ref[...], BRANCH).astype(F32)
    meta_ref[me] = jnp.zeros(meta_ref.shape[1:], F32)
    meta_ref[me, 0:1, 0:scen] = weight_row
    meta_ref[me, 1:2, 0:scen] = branch_row
    sec_tab[quarter] = ps_ref[...].astype(F32)
    pl.semaphore_wait(barrier, n - 1)

    third_far = remote(
        pt_hbm, pt_tab.at[quarter], pt_ssem.at[0], pt_rsem.at[0], far_peer
    )
    third_core = remote(
        pt_hbm, pt_tab.at[quarter], pt_ssem.at[1], pt_rsem.at[1], core_peer
    )
    third_pass = remote(
        pt_tab.at[far_q], pt_tab.at[far_q], pt_ssem.at[2], pt_rsem.at[2], core_peer
    )
    third_far.start()
    third_core.start()

    def meta_copy(r):
        return remote(
            meta_ref.at[me],
            meta_ref.at[me],
            meta_ssem.at[r],
            meta_rsem.at[r],
            lax.rem(me + r, n),
        )

    @pl.loop(1, n)
    def _(r):
        meta_copy(r).start()

    def sec_copy(r):
        return remote(
            sec_tab.at[quarter],
            sec_tab.at[quarter],
            sec_ssem.at[r],
            sec_rsem.at[r],
            base + lax.rem(quarter + r, 4),
        )

    for r in range(1, 4):
        sec_copy(r).start()

    lane = lax.broadcasted_iota(jnp.int32, (scen, rows), 1)
    low = lax.broadcasted_iota(jnp.int32, (scen, rows), 0) * hours
    spread = jnp.where((lane >= low) & (lane < low + hours), 1.0, 0.0).astype(BF16)
    small = jnp.concatenate(
        (
            weight_row,
            branch_row,
            lax.broadcasted_iota(jnp.int32, (1, scen), 1).astype(F32),
            jnp.zeros((5, scen), F32),
        ),
        axis=0,
    ).astype(BF16)
    wide = jnp.dot(small, spread, preferred_element_type=F32)
    hour = lax.broadcasted_iota(jnp.int32, (1, rows), 1).astype(F32) - hours * wide[2:3]
    place = hour + jnp.where(hour >= 2.0 * hs, hs * wide[1:2], 0.0)
    line = lax.broadcasted_iota(jnp.int32, w_mat.shape, 0).astype(F32)
    w_mat[...] = jnp.where(place == line, wide[0:1], 0.0).astype(BF16)

    def x1_copy(k):
        return remote(
            x1_send.at[k], x1_recv.at[k], x1_ssem.at[k], x1_rsem.at[k], core_peer
        )

    def x2_copy(k):
        return remote(
            x2_send.at[k], x2_recv.at[k], x2_ssem.at[k], x2_rsem.at[k], far_peer
        )

    own_rows = pl.ds(pl.multiple_of(2 * hs + half * core, 16), half)
    peer_rows = pl.ds(pl.multiple_of(2 * hs + half * (1 - core), 16), half)
    for k in range(CHUNKS):
        load(k, 0).wait()
        load(k, 1).wait()
        s_ref[:, chunk(k)] = jnp.dot(
            w_mat[...], c_ref[:, chunk(k)], preferred_element_type=F32
        ) + jnp.dot(w_mat[...], d_ref[:, chunk(k)], preferred_element_type=F32)
        x1_send[k] = s_ref[peer_rows, chunk(k)].astype(BF16)
        x1_copy(k).start()
    for j in range(4):
        fs_send[j] = s_ref[0 : 2 * hs, j * quart : (j + 1) * quart].astype(BF16)

    def fs_copy(r):
        to = lax.rem(quarter + r, 4)
        return remote(
            fs_send.at[to], fs_recv.at[r], fs_ssem.at[r], fs_rsem.at[r], base + to
        )

    for r in range(1, 4):
        fs_copy(r).start()

    third_far.wait_recv()
    third_pass.start()

    for k in range(CHUNKS):
        x1_copy(k).wait_recv()
        s_ref[own_rows, chunk(k)] = s_ref[own_rows, chunk(k)] + x1_recv[k].astype(F32)
        x2_send[k] = s_ref[own_rows, chunk(k)].astype(BF16)
        x2_copy(k).start()

    my_cols = pl.ds(pl.multiple_of(quarter * quart, 128), quart)
    pair = s_ref[0 : 2 * hs, my_cols]
    for r in range(1, 4):
        fs_copy(r).wait_recv()
        pair = pair + fs_recv[r].astype(F32)
    z_ref[team] = pair[0:hs]

    def z_copy(r):
        return remote(
            z_ref.at[team],
            z_ref.at[team],
            z_ssem.at[r],
            z_rsem.at[r],
            lax.rem(team + r, groups2) * 4 + quarter,
        )

    for r in range(1, groups2):
        z_copy(r).start()

    tab_ref[0] = pf_ref[...].astype(F32)
    for r in range(1, 4):
        sec_copy(r).wait_recv()
    for j in range(4):
        tab_ref[1, :, j * quart : (j + 1) * quart] = sec_tab[j]
    own_third.wait()
    third_core.wait_recv()
    third_pass.wait_recv()
    for j in range(4):
        tab_ref[2 + 4 * j : 6 + 4 * j] = pt_tab[j].astype(F32).reshape(4, hs, cols)

    @pl.loop(0, scen // 2)
    def _(i):
        window = pl.ds(pl.multiple_of(i * 2 * hours, 16), 2 * hours)
        b0 = lax.rem(b_smem[2 * i], BRANCH)
        b1 = lax.rem(b_smem[2 * i + 1], BRANCH)
        for k in range(CHUNKS):
            first = tab_ref[0, :, chunk(k)]
            second = tab_ref[1, :, chunk(k)]
            anchor = jnp.concatenate(
                (
                    first,
                    second,
                    tab_ref[2 + b0, :, chunk(k)],
                    first,
                    second,
                    tab_ref[2 + b1, :, chunk(k)],
                ),
                axis=0,
            )
            t_ref[window, chunk(k)] = (
                PENALTY * anchor
                - c_ref[window, chunk(k)].astype(F32)
                - d_ref[window, chunk(k)].astype(F32)
            ).astype(BF16)

    cost_ref[...] = jnp.zeros_like(cost_ref)

    def product(k):
        load(k, 2).wait()

        @pl.loop(0, width // tile)
        def _(j):
            part = pl.ds(pl.multiple_of(k * width + j * tile, 128), tile)
            x = jnp.dot(t_ref[...], inv_ref[:, part], preferred_element_type=F32)
            x_ref[:, part] = x
            y = x * c_ref[:, part].astype(F32)
            cost = cost_ref[...]
            for e in range(tile // 128):
                cost = cost + y[:, e * 128 : (e + 1) * 128]
            cost_ref[...] = cost

    product(0)

    @pl.loop(1, n)
    def _(r):
        meta_copy(r).wait_recv()

    mass_all = jnp.sum(meta_ref[:, 0, :])
    mass_two = jnp.zeros((), F32)
    node_line = lax.broadcasted_iota(jnp.int32, (BRANCH * hs, 128), 0).astype(F32)
    mass_lanes = jnp.zeros((BRANCH * hs, 128), F32)
    for j in range(4):
        w_j = meta_ref[base + j, 0:1, :]
        b_j = meta_ref[base + j, 1:2, :] * hs
        mass_two = mass_two + jnp.sum(w_j)
        mass_lanes = mass_lanes + jnp.where(
            (node_line >= b_j) & (node_line < b_j + hs), w_j, 0.0
        )
    s_ref[2 * hs :, cols : cols + 128] = jnp.broadcast_to(
        jnp.sum(mass_lanes, axis=1, keepdims=True), mass_lanes.shape
    )
    for r in range(1, groups2):
        z_copy(r).wait_recv()
    total = z_ref[0]
    for g in range(1, groups2):
        total = total + z_ref[g]
    tl_ref[0 : 2 * hs, my_cols] = jnp.concatenate(
        (
            PENALTY * tab_ref[0, :, my_cols] - total / mass_all,
            PENALTY * tab_ref[1, :, my_cols] - pair[hs:] / mass_two,
        ),
        axis=0,
    ).astype(BF16)

    def ag_copy(r):
        return remote(
            tl_ref.at[0 : 2 * hs, my_cols],
            tl_ref.at[0 : 2 * hs, my_cols],
            ag_ssem.at[r],
            ag_rsem.at[r],
            base + lax.rem(quarter + r, 4),
        )

    for r in range(1, 4):
        ag_copy(r).start()

    for k in range(1, CHUNKS):
        product(k)

    by_scen = jnp.sum(cost_ref[...].reshape(scen, hours, 128), axis=1)
    cost_row = lax.dot_general(
        jnp.ones((8, 128), F32),
        by_scen,
        (((1,), (1,)), ((), ())),
        precision=lax.Precision.HIGHEST,
        preferred_element_type=F32,
    )[0:1] / (hours * cols)
    low_end = em_ref[0] - (CVAR_WEIGHT + ed_ref[...]) / PENALTY
    high_end = low_end + CVAR_WEIGHT / ((1.0 - CVAR_LEVEL) * PENALTY)
    eta = jnp.minimum(jnp.maximum(cost_row, low_end), high_end)
    eta_ref[me] = jnp.broadcast_to(
        jnp.sum(weight_row * eta, axis=1, keepdims=True), eta_ref.shape[1:]
    )

    def eta_copy(r):
        return remote(
            eta_ref.at[me],
            eta_ref.at[me],
            eta_ssem.at[r],
            eta_rsem.at[r],
            lax.rem(me + r, n),
        )

    @pl.loop(1, n)
    def _(r):
        eta_copy(r).start()

    def x3_copy(k):
        return remote(
            tl_ref.at[own_rows, chunk(k)],
            tl_ref.at[own_rows, chunk(k)],
            x3_ssem.at[k],
            x3_rsem.at[k],
            core_peer,
        )

    own_mass = s_ref[own_rows, cols : cols + 1]
    own_nodes = pl.ds(2 + (BRANCH // 2) * core, BRANCH // 2)
    for k in range(CHUNKS):
        x2_copy(k).wait_recv()
        mean = (s_ref[own_rows, chunk(k)] + x2_recv[k].astype(F32)) / own_mass
        anchor = tab_ref[own_nodes, :, chunk(k)].reshape(half, width)
        tl_ref[own_rows, chunk(k)] = (PENALTY * anchor - mean).astype(BF16)
        x3_copy(k).start()
    for r in range(1, 4):
        ag_copy(r).wait_recv()
    for k in range(CHUNKS):
        x3_copy(k).wait_recv()

    @pl.loop(0, cols // tile)
    def _(j):
        part = pl.ds(pl.multiple_of(j * tile, 128), tile)
        avg_ref[:, :, part] = jnp.dot(
            tl_ref[...], inv_ref[:, part], preferred_element_type=F32
        ).reshape(avg_ref.shape[0], hs, tile)

    @pl.loop(0, scen // 2)
    def _(i):
        window = pl.ds(pl.multiple_of(i * 2 * hours, 16), 2 * hours)
        b0 = lax.rem(b_smem[2 * i], BRANCH)
        b1 = lax.rem(b_smem[2 * i + 1], BRANCH)
        for k in range(CHUNKS):
            first = avg_ref[0, :, chunk(k)]
            second = avg_ref[1, :, chunk(k)]
            mean = jnp.concatenate(
                (
                    first,
                    second,
                    avg_ref[2 + b0, :, chunk(k)],
                    first,
                    second,
                    avg_ref[2 + b1, :, chunk(k)],
                ),
                axis=0,
            )
            duals_ref[window, chunk(k)] = (
                d_ref[window, chunk(k)].astype(F32)
                + PENALTY * (x_ref[window, chunk(k)] - mean)
            ).astype(BF16)

    first_ref[...] = avg_ref[0]
    second_ref[...] = avg_ref[1, :, my_cols]
    third_ref[...] = avg_ref[pl.ds(2 + 4 * quarter, 4)].reshape(4 * hs, cols)

    @pl.loop(1, n)
    def _(r):
        eta_copy(r).wait_recv()

    level = eta_ref[0]
    for g in range(1, n):
        level = level + eta_ref[g]
    level = level / mass_all
    level_ref[...] = level[0:1, 0:1]
    ednew_ref[...] = ed_ref[...] + PENALTY * (eta - level[0:1, 0:scen])

    @pl.loop(1, n)
    def _(r):
        meta_copy(r).wait_send()
        eta_copy(r).wait_send()

    for copy in (third_far, third_core, third_pass):
        copy.wait_send()
    for r in range(1, 4):
        sec_copy(r).wait_send()
        fs_copy(r).wait_send()
        ag_copy(r).wait_send()
    for r in range(1, groups2):
        z_copy(r).wait_send()
    for k in range(CHUNKS):
        x1_copy(k).wait_send()
        x2_copy(k).wait_send()
        x3_copy(k).wait_send()


def body(
    n,
    unit_costs,
    hour_duals,
    inverse,
    weights,
    section_three,
    prev_first,
    prev_second,
    prev_third,
    eta_mean,
    eta_duals,
):
    scen, hours, cols = unit_costs.shape
    hs = hours // 3
    rows = scen * hours
    lines = 2 * hs + BRANCH * hs
    width, quart = cols // CHUNKS, cols // 4
    half = BRANCH * hs // 2
    vmem = pl.BlockSpec(memory_space=pltpu.VMEM)
    smem = pl.BlockSpec(memory_space=pltpu.SMEM)
    anywhere = pl.BlockSpec(memory_space=pl.ANY)
    dma = pltpu.SemaphoreType.DMA
    outs = pl.pallas_call(
        functools.partial(kernel, n),
        out_shape=(
            jax.ShapeDtypeStruct((rows, cols), BF16),
            jax.ShapeDtypeStruct((hs, cols), F32),
            jax.ShapeDtypeStruct((hs, quart), F32),
            jax.ShapeDtypeStruct((4 * hs, cols), F32),
            jax.ShapeDtypeStruct((1, 1), F32),
            jax.ShapeDtypeStruct((1, scen), F32),
        ),
        in_specs=[
            anywhere,
            anywhere,
            anywhere,
            vmem,
            vmem,
            smem,
            vmem,
            vmem,
            anywhere,
            smem,
            vmem,
        ],
        out_specs=(vmem,) * 6,
        scratch_shapes=[
            pltpu.VMEM((rows, cols), BF16),
            pltpu.VMEM((rows, cols), BF16),
            pltpu.VMEM((cols, cols), BF16),
            pltpu.VMEM((rows, cols), BF16),
            pltpu.VMEM((rows, cols), F32),
            pltpu.VMEM((lines, cols + 128), F32),
            pltpu.VMEM((lines, rows), BF16),
            pltpu.VMEM((lines // hs, hs, cols), F32),
            pltpu.VMEM((lines // hs, hs, cols), F32),
            pltpu.VMEM((lines, cols), BF16),
            pltpu.VMEM((4, 4 * hs, cols), BF16),
            pltpu.VMEM((4, hs, quart), F32),
            pltpu.VMEM((n, 8, 128), F32),
            pltpu.VMEM((n, 8, 128), F32),
            pltpu.VMEM((CHUNKS, half, width), BF16),
            pltpu.VMEM((CHUNKS, half, width), BF16),
            pltpu.VMEM((CHUNKS, half, width), BF16),
            pltpu.VMEM((CHUNKS, half, width), BF16),
            pltpu.VMEM((4, 2 * hs, quart), BF16),
            pltpu.VMEM((4, 2 * hs, quart), BF16),
            pltpu.VMEM((n // 4, hs, quart), F32),
            pltpu.VMEM((rows, 128), F32),
            dma((4, CHUNKS)),
            dma((n,)),
            dma((n,)),
            dma((n,)),
            dma((n,)),
            dma((3,)),
            dma((3,)),
            dma((4,)),
            dma((4,)),
            dma((CHUNKS,)),
            dma((CHUNKS,)),
            dma((CHUNKS,)),
            dma((CHUNKS,)),
            dma((CHUNKS,)),
            dma((CHUNKS,)),
            dma((4,)),
            dma((4,)),
            dma((n // 4,)),
            dma((n // 4,)),
            dma((4,)),
            dma((4,)),
        ],
        compiler_params=pltpu.CompilerParams(
            collective_id=0, has_side_effects=True, vmem_limit_bytes=52 * 2**20
        ),
    )(
        unit_costs.reshape(rows, cols),
        hour_duals.reshape(rows, cols),
        inverse,
        weights.reshape(1, scen),
        section_three.reshape(1, scen),
        section_three,
        prev_first,
        prev_second.reshape(hs, quart),
        prev_third.reshape(4 * hs, cols),
        eta_mean,
        eta_duals.reshape(1, scen),
    )
    duals_new, first_avg, second_avg, third_avg, level, eta_new = outs
    return (
        duals_new.reshape(scen, hours, cols),
        first_avg,
        second_avg.reshape(1, hs, quart),
        third_avg.reshape(4, hs, cols),
        level.reshape(1),
        eta_new.reshape(scen),
    )


def solution(mesh):
    both = ("groups", "node")
    cube = P(both, None, None)
    in_specs = (
        cube,
        cube,
        P(),
        P(both),
        P(both),
        P("groups", None),
        cube,
        cube,
        P("groups"),
        P(both),
    )
    out_specs = (cube, P("groups", None), cube, cube, P("groups"), P(both))
    return jax.shard_map(
        functools.partial(body, mesh.shape["node"]),
        mesh=mesh,
        in_specs=in_specs,
        out_specs=out_specs,
        check_vma=False,
    )
```

```python
import functools

import jax
import jax.numpy as jnp
from jax import lax
from jax.experimental import pallas as pl
from jax.experimental.pallas import tpu as pltpu
from jax.sharding import PartitionSpec as P

BRANCH = 16
PENALTY = 1.0
CVAR_WEIGHT = 0.25
CVAR_LEVEL = 0.75
CHUNKS = 4
MESH = pl.DeviceIdType.MESH
F32 = jnp.float32
BF16 = jnp.bfloat16


def kernel(
    n,
    c_hbm,
    d_hbm,
    inv_hbm,
    w_hbm,
    b_hbm,
    b_smem,
    pf_hbm,
    ps_hbm,
    pt_hbm,
    em_ref,
    ed_hbm,
    x_ref,
    avg_ref,
    second_ref,
    third_ref,
    level_ref,
    ednew_ref,
    c_ref,
    d_ref,
    inv_ref,
    t_ref,
    s_ref,
    w_mat,
    tab_ref,
    tl_ref,
    pt_tab,
    sec_tab,
    meta_ref,
    eta_ref,
    x1_send,
    x1_recv,
    x2_send,
    x2_recv,
    fs_send,
    fs_recv,
    z_ref,
    cost_ref,
    w_ref,
    b_ref,
    pf_ref,
    ps_ref,
    ed_ref,
    load_sem,
    small_sem,
    meta_ssem,
    meta_rsem,
    eta_ssem,
    eta_rsem,
    pt_ssem,
    pt_rsem,
    sec_ssem,
    sec_rsem,
    x1_ssem,
    x1_rsem,
    x2_ssem,
    x2_rsem,
    x3_ssem,
    x3_rsem,
    fs_ssem,
    fs_rsem,
    z_ssem,
    z_rsem,
    ag_ssem,
    ag_rsem,
):
    rows, cols = c_ref.shape
    scen = b_smem.shape[0]
    hours = rows // scen
    hs = hours // 3
    groups2 = n // 4
    width = cols // CHUNKS
    quart = cols // 4
    tile = min(256, width)
    half = BRANCH * hs // 2
    me = lax.axis_index("node")
    quarter = lax.rem(me, 4)
    core = lax.rem(me, 2)
    base = me - quarter
    team = lax.div(me, 4)
    core_peer = me + 1 - 2 * core
    far_peer = me + 2 - 4 * lax.rem(lax.div(me, 2), 2)
    far_q = lax.rem(quarter + 2, 4)
    core_q = quarter + 1 - 2 * core
    diag_q = lax.rem(core_q + 2, 4)

    def remote(src, dst, ssem, rsem, device):
        return pltpu.make_async_remote_copy(
            src_ref=src,
            dst_ref=dst,
            send_sem=ssem,
            recv_sem=rsem,
            device_id={"node": device},
            device_id_type=MESH,
        )

    def chunk(k):
        return pl.ds(k * width, width)

    def load(k, which):
        src, dst = ((c_hbm, c_ref), (d_hbm, d_ref), (inv_hbm, inv_ref))[which]
        return pltpu.make_async_copy(
            src.at[:, chunk(k)], dst.at[:, chunk(k)], load_sem.at[which, k]
        )

    def fetch(k):
        src, dst = (
            (w_hbm, w_ref),
            (b_hbm, b_ref),
            (ps_hbm, ps_ref),
            (pf_hbm, pf_ref),
            (ed_hbm, ed_ref),
        )[k]
        return pltpu.make_async_copy(src, dst, small_sem.at[k])

    for k in range(5):
        fetch(k).start()
    for k in range(CHUNKS):
        load(k, 0).start()
        load(k, 1).start()
    for k in range(CHUNKS):
        load(k, 2).start()
    own_third = pltpu.make_async_copy(pt_hbm, pt_tab.at[quarter], load_sem.at[3, 0])
    own_third.start()

    barrier = pltpu.get_barrier_semaphore()

    @pl.loop(1, n)
    def _(r):
        pl.semaphore_signal(
            barrier, inc=1, device_id={"node": lax.rem(me + r, n)}, device_id_type=MESH
        )

    for k in range(5):
        fetch(k).wait()
    weight_row = w_ref[...].astype(F32)
    branch_row = lax.rem(b_ref[...], BRANCH).astype(F32)
    meta_ref[me] = jnp.zeros(meta_ref.shape[1:], F32)
    meta_ref[me, 0:1, 0:scen] = weight_row
    meta_ref[me, 1:2, 0:scen] = branch_row
    sec_tab[quarter] = ps_ref[...].astype(F32)
    pl.semaphore_wait(barrier, n - 1)

    third_far = remote(
        pt_hbm, pt_tab.at[quarter], pt_ssem.at[0], pt_rsem.at[0], far_peer
    )
    third_core = remote(
        pt_hbm, pt_tab.at[quarter], pt_ssem.at[1], pt_rsem.at[1], core_peer
    )
    third_pass = remote(
        pt_tab.at[far_q], pt_tab.at[far_q], pt_ssem.at[2], pt_rsem.at[2], core_peer
    )
    third_far.start()
    third_core.start()

    def meta_copy(r):
        return remote(
            meta_ref.at[me],
            meta_ref.at[me],
            meta_ssem.at[r],
            meta_rsem.at[r],
            lax.rem(me + r, n),
        )

    @pl.loop(1, n)
    def _(r):
        meta_copy(r).start()

    def sec_copy(r):
        return remote(
            sec_tab.at[quarter],
            sec_tab.at[quarter],
            sec_ssem.at[r],
            sec_rsem.at[r],
            base + lax.rem(quarter + r, 4),
        )

    for r in range(1, 4):
        sec_copy(r).start()

    lane = lax.broadcasted_iota(jnp.int32, (scen, rows), 1)
    low = lax.broadcasted_iota(jnp.int32, (scen, rows), 0) * hours
    spread = jnp.where((lane >= low) & (lane < low + hours), 1.0, 0.0).astype(BF16)
    small = jnp.concatenate(
        (
            weight_row,
            branch_row,
            lax.broadcasted_iota(jnp.int32, (1, scen), 1).astype(F32),
            jnp.zeros((5, scen), F32),
        ),
        axis=0,
    ).astype(BF16)
    wide = jnp.dot(small, spread, preferred_element_type=F32)
    hour = lax.broadcasted_iota(jnp.int32, (1, rows), 1).astype(F32) - hours * wide[2:3]
    place = hour + jnp.where(hour >= 2.0 * hs, hs * wide[1:2], 0.0)
    line = lax.broadcasted_iota(jnp.int32, w_mat.shape, 0).astype(F32)
    w_mat[...] = jnp.where(place == line, wide[0:1], 0.0).astype(BF16)

    def x1_copy(k):
        return remote(
            x1_send.at[k], x1_recv.at[k], x1_ssem.at[k], x1_rsem.at[k], core_peer
        )

    def x2_copy(k):
        return remote(
            x2_send.at[k], x2_recv.at[k], x2_ssem.at[k], x2_rsem.at[k], far_peer
        )

    own_rows = pl.ds(pl.multiple_of(2 * hs + half * core, 16), half)
    peer_rows = pl.ds(pl.multiple_of(2 * hs + half * (1 - core), 16), half)
    for k in range(CHUNKS):
        load(k, 0).wait()
        load(k, 1).wait()
        s_ref[:, chunk(k)] = jnp.dot(
            w_mat[...], c_ref[:, chunk(k)], preferred_element_type=F32
        ) + jnp.dot(w_mat[...], d_ref[:, chunk(k)], preferred_element_type=F32)
        x1_send[k] = s_ref[peer_rows, chunk(k)].astype(BF16)
        x1_copy(k).start()
    for j in range(4):
        fs_send[j] = s_ref[0 : 2 * hs, j * quart : (j + 1) * quart]

    def fs_copy(r):
        to = lax.rem(quarter + r, 4)
        return remote(
            fs_send.at[to], fs_recv.at[r], fs_ssem.at[r], fs_rsem.at[r], base + to
        )

    for r in range(1, 4):
        fs_copy(r).start()

    third_far.wait_recv()
    third_pass.start()

    for k in range(CHUNKS):
        x1_copy(k).wait_recv()
        s_ref[own_rows, chunk(k)] = s_ref[own_rows, chunk(k)] + x1_recv[k].astype(F32)
        x2_send[k] = s_ref[own_rows, chunk(k)].astype(BF16)
        x2_copy(k).start()

    my_cols = pl.ds(pl.multiple_of(quarter * quart, 128), quart)
    pair = s_ref[0 : 2 * hs, my_cols]
    for r in range(1, 4):
        fs_copy(r).wait_recv()
        pair = pair + fs_recv[r]
    z_ref[team] = pair[0:hs]

    def z_copy(r):
        return remote(
            z_ref.at[team],
            z_ref.at[team],
            z_ssem.at[r],
            z_rsem.at[r],
            lax.rem(team + r, groups2) * 4 + quarter,
        )

    for r in range(1, groups2):
        z_copy(r).start()

    tab_ref[0] = pf_ref[...].astype(F32)
    for r in range(1, 4):
        sec_copy(r).wait_recv()
    for j in range(4):
        tab_ref[1, :, j * quart : (j + 1) * quart] = sec_tab[j]
    own_third.wait()
    third_core.wait_recv()
    third_pass.wait_recv()
    for j in range(4):
        tab_ref[2 + 4 * j : 6 + 4 * j] = pt_tab[j].astype(F32).reshape(4, hs, cols)

    @pl.loop(0, scen // 2)
    def _(i):
        window = pl.ds(pl.multiple_of(i * 2 * hours, 16), 2 * hours)
        b0 = lax.rem(b_smem[2 * i], BRANCH)
        b1 = lax.rem(b_smem[2 * i + 1], BRANCH)
        for k in range(CHUNKS):
            first = tab_ref[0, :, chunk(k)]
            second = tab_ref[1, :, chunk(k)]
            anchor = jnp.concatenate(
                (
                    first,
                    second,
                    tab_ref[2 + b0, :, chunk(k)],
                    first,
                    second,
                    tab_ref[2 + b1, :, chunk(k)],
                ),
                axis=0,
            )
            t_ref[window, chunk(k)] = (
                PENALTY * anchor
                - c_ref[window, chunk(k)].astype(F32)
                - d_ref[window, chunk(k)].astype(F32)
            ).astype(BF16)

    cost_ref[...] = jnp.zeros_like(cost_ref)

    def product(k):
        load(k, 2).wait()

        @pl.loop(0, width // tile)
        def _(j):
            part = pl.ds(pl.multiple_of(k * width + j * tile, 128), tile)
            x = jnp.dot(t_ref[...], inv_ref[:, part], preferred_element_type=F32)
            x_ref[:, part] = x
            y = x * c_ref[:, part].astype(F32)
            cost = cost_ref[...]
            for e in range(tile // 128):
                cost = cost + y[:, e * 128 : (e + 1) * 128]
            cost_ref[...] = cost

    product(0)

    @pl.loop(1, n)
    def _(r):
        meta_copy(r).wait_recv()

    mass_all = jnp.sum(meta_ref[:, 0, :])
    mass_two = jnp.zeros((), F32)
    node_line = lax.broadcasted_iota(jnp.int32, (BRANCH * hs, 128), 0).astype(F32)
    mass_lanes = jnp.zeros((BRANCH * hs, 128), F32)
    for j in range(4):
        w_j = meta_ref[base + j, 0:1, :]
        b_j = meta_ref[base + j, 1:2, :] * hs
        mass_two = mass_two + jnp.sum(w_j)
        mass_lanes = mass_lanes + jnp.where(
            (node_line >= b_j) & (node_line < b_j + hs), w_j, 0.0
        )
    s_ref[2 * hs :, cols : cols + 128] = jnp.broadcast_to(
        jnp.sum(mass_lanes, axis=1, keepdims=True), mass_lanes.shape
    )
    for r in range(1, groups2):
        z_copy(r).wait_recv()
    total = z_ref[0]
    for g in range(1, groups2):
        total = total + z_ref[g]
    tl_ref[0 : 2 * hs, my_cols] = jnp.concatenate(
        (
            PENALTY * tab_ref[0, :, my_cols] - total / mass_all,
            PENALTY * tab_ref[1, :, my_cols] - pair[hs:] / mass_two,
        ),
        axis=0,
    ).astype(BF16)

    def ag_copy(r):
        return remote(
            tl_ref.at[0 : 2 * hs, my_cols],
            tl_ref.at[0 : 2 * hs, my_cols],
            ag_ssem.at[r],
            ag_rsem.at[r],
            base + lax.rem(quarter + r, 4),
        )

    for r in range(1, 4):
        ag_copy(r).start()

    for k in range(1, CHUNKS):
        product(k)

    by_scen = jnp.sum(cost_ref[...].reshape(scen, hours, 128), axis=1)
    cost_row = lax.dot_general(
        jnp.ones((8, 128), F32),
        by_scen,
        (((1,), (1,)), ((), ())),
        precision=lax.Precision.HIGHEST,
        preferred_element_type=F32,
    )[0:1] / (hours * cols)
    low_end = em_ref[0] - (CVAR_WEIGHT + ed_ref[...]) / PENALTY
    high_end = low_end + CVAR_WEIGHT / ((1.0 - CVAR_LEVEL) * PENALTY)
    eta = jnp.minimum(jnp.maximum(cost_row, low_end), high_end)
    eta_ref[me] = jnp.broadcast_to(
        jnp.sum(weight_row * eta, axis=1, keepdims=True), eta_ref.shape[1:]
    )

    def eta_copy(r):
        return remote(
            eta_ref.at[me],
            eta_ref.at[me],
            eta_ssem.at[r],
            eta_rsem.at[r],
            lax.rem(me + r, n),
        )

    @pl.loop(1, n)
    def _(r):
        eta_copy(r).start()

    def x3_copy(k):
        return remote(
            tl_ref.at[own_rows, chunk(k)],
            tl_ref.at[own_rows, chunk(k)],
            x3_ssem.at[k],
            x3_rsem.at[k],
            core_peer,
        )

    own_mass = s_ref[own_rows, cols : cols + 1]
    own_nodes = pl.ds(2 + (BRANCH // 2) * core, BRANCH // 2)
    for k in range(CHUNKS):
        x2_copy(k).wait_recv()
        mean = (s_ref[own_rows, chunk(k)] + x2_recv[k].astype(F32)) / own_mass
        anchor = tab_ref[own_nodes, :, chunk(k)].reshape(half, width)
        tl_ref[own_rows, chunk(k)] = (PENALTY * anchor - mean).astype(BF16)
        x3_copy(k).start()
    for r in range(1, 4):
        ag_copy(r).wait_recv()
    for k in range(CHUNKS):
        x3_copy(k).wait_recv()

    @pl.loop(0, cols // tile)
    def _(j):
        part = pl.ds(pl.multiple_of(j * tile, 128), tile)
        avg_ref[:, :, part] = jnp.dot(
            tl_ref[...], inv_ref[:, part], preferred_element_type=F32
        ).reshape(avg_ref.shape[0], hs, tile)

    second_ref[...] = avg_ref[1, :, my_cols]
    third_ref[...] = avg_ref[pl.ds(2 + 4 * quarter, 4)].reshape(4 * hs, cols)

    @pl.loop(1, n)
    def _(r):
        eta_copy(r).wait_recv()

    level = eta_ref[0]
    for g in range(1, n):
        level = level + eta_ref[g]
    level = level / mass_all
    level_ref[...] = level[0:1, 0:1]
    ednew_ref[...] = ed_ref[...] + PENALTY * (eta - level[0:1, 0:scen])

    @pl.loop(1, n)
    def _(r):
        meta_copy(r).wait_send()
        eta_copy(r).wait_send()

    for copy in (third_far, third_core, third_pass):
        copy.wait_send()
    for r in range(1, 4):
        sec_copy(r).wait_send()
        fs_copy(r).wait_send()
        ag_copy(r).wait_send()
    for r in range(1, groups2):
        z_copy(r).wait_send()
    for k in range(CHUNKS):
        x1_copy(k).wait_send()
        x2_copy(k).wait_send()
        x3_copy(k).wait_send()


def finish(
    b_smem,
    x_ref,
    d_ref,
    avg_ref,
    second_in,
    third_in,
    level_in,
    ednew_in,
    duals_ref,
    first_ref,
    second_ref,
    third_ref,
    level_ref,
    ednew_ref,
):
    step = pl.program_id(0)
    cols = x_ref.shape[1]
    hours = 3 * avg_ref.shape[1]
    pairs = x_ref.shape[0] // (2 * hours)
    width = cols // CHUNKS

    @pl.when(step == 0)
    def _():
        first_ref[...] = avg_ref[0]
        second_ref[...] = second_in[...]
        third_ref[...] = third_in[...]
        level_ref[...] = level_in[...]
        ednew_ref[...] = ednew_in[...]

    for i in range(pairs):
        window = slice(i * 2 * hours, (i + 1) * 2 * hours)
        b0 = lax.rem(b_smem[2 * (step * pairs + i)], BRANCH)
        b1 = lax.rem(b_smem[2 * (step * pairs + i) + 1], BRANCH)
        for k in range(CHUNKS):
            part = slice(k * width, (k + 1) * width)
            first = avg_ref[0, :, part]
            second = avg_ref[1, :, part]
            mean = jnp.concatenate(
                (
                    first,
                    second,
                    avg_ref[2 + b0, :, part],
                    first,
                    second,
                    avg_ref[2 + b1, :, part],
                ),
                axis=0,
            )
            duals_ref[window, part] = (
                d_ref[window, part].astype(F32)
                + PENALTY * (x_ref[window, part] - mean)
            ).astype(BF16)


def stay(value):
    return pltpu.with_memory_space_constraint(value, pltpu.HBM)


def body(
    n,
    unit_costs,
    hour_duals,
    inverse,
    weights,
    section_three,
    prev_first,
    prev_second,
    prev_third,
    eta_mean,
    eta_duals,
):
    scen, hours, cols = unit_costs.shape
    hs = hours // 3
    rows = scen * hours
    lines = 2 * hs + BRANCH * hs
    width, quart = cols // CHUNKS, cols // 4
    half = BRANCH * hs // 2
    vmem = pl.BlockSpec(memory_space=pltpu.VMEM)
    smem = pl.BlockSpec(memory_space=pltpu.SMEM)
    hbm = pl.BlockSpec(memory_space=pltpu.HBM)
    dma = pltpu.SemaphoreType.DMA
    outs = pl.pallas_call(
        functools.partial(kernel, n),
        out_shape=(
            jax.ShapeDtypeStruct((rows, cols), F32),
            jax.ShapeDtypeStruct((lines // hs, hs, cols), F32),
            jax.ShapeDtypeStruct((hs, quart), F32),
            jax.ShapeDtypeStruct((4 * hs, cols), F32),
            jax.ShapeDtypeStruct((1, 1), F32),
            jax.ShapeDtypeStruct((1, scen), F32),
        ),
        in_specs=[
            hbm,
            hbm,
            hbm,
            hbm,
            hbm,
            smem,
            hbm,
            hbm,
            hbm,
            smem,
            hbm,
        ],
        out_specs=(vmem,) * 6,
        scratch_shapes=[
            pltpu.VMEM((rows, cols), BF16),
            pltpu.VMEM((rows, cols), BF16),
            pltpu.VMEM((cols, cols), BF16),
            pltpu.VMEM((rows, cols), BF16),
            pltpu.VMEM((lines, cols + 128), F32),
            pltpu.VMEM((lines, rows), BF16),
            pltpu.VMEM((lines // hs, hs, cols), F32),
            pltpu.VMEM((lines, cols), BF16),
            pltpu.VMEM((4, 4 * hs, cols), BF16),
            pltpu.VMEM((4, hs, quart), F32),
            pltpu.VMEM((n, 8, 128), F32),
            pltpu.VMEM((n, 8, 128), F32),
            pltpu.VMEM((CHUNKS, half, width), BF16),
            pltpu.VMEM((CHUNKS, half, width), BF16),
            pltpu.VMEM((CHUNKS, half, width), BF16),
            pltpu.VMEM((CHUNKS, half, width), BF16),
            pltpu.VMEM((4, 2 * hs, quart), F32),
            pltpu.VMEM((4, 2 * hs, quart), F32),
            pltpu.VMEM((n // 4, hs, quart), F32),
            pltpu.VMEM((rows, 128), F32),
            pltpu.VMEM((1, scen), jnp.int32),
            pltpu.VMEM((1, scen), jnp.int32),
            pltpu.VMEM((hs, cols), BF16),
            pltpu.VMEM((hs, quart), BF16),
            pltpu.VMEM((1, scen), F32),
            dma((4, CHUNKS)),
            dma((5,)),
            dma((n,)),
            dma((n,)),
            dma((n,)),
            dma((n,)),
            dma((3,)),
            dma((3,)),
            dma((4,)),
            dma((4,)),
            dma((CHUNKS,)),
            dma((CHUNKS,)),
            dma((CHUNKS,)),
            dma((CHUNKS,)),
            dma((CHUNKS,)),
            dma((CHUNKS,)),
            dma((4,)),
            dma((4,)),
            dma((n // 4,)),
            dma((n // 4,)),
            dma((4,)),
            dma((4,)),
        ],
        compiler_params=pltpu.CompilerParams(
            collective_id=0, has_side_effects=True, vmem_limit_bytes=40 * 2**20
        ),
    )(
        stay(unit_costs.reshape(rows, cols)),
        stay(hour_duals.reshape(rows, cols)),
        stay(inverse),
        stay(weights.reshape(1, scen)),
        stay(section_three.reshape(1, scen)),
        section_three,
        stay(prev_first),
        stay(prev_second.reshape(hs, quart)),
        stay(prev_third.reshape(4 * hs, cols)),
        eta_mean,
        stay(eta_duals.reshape(1, scen)),
    )
    steps = max(k for k in (1, 2, 4) if scen % (2 * k) == 0)
    block = rows // steps

    def fixed(*shape):
        return pl.BlockSpec(shape, lambda i: (0,) * len(shape))

    moving = pl.BlockSpec((block, cols), lambda i: (i, 0))
    smalls = (fixed(hs, quart), fixed(4 * hs, cols), fixed(1, 1), fixed(1, scen))
    duals_new, first_avg, second_avg, third_avg, level, eta_new = pl.pallas_call(
        finish,
        grid=(steps,),
        out_shape=(
            jax.ShapeDtypeStruct((rows, cols), BF16),
            jax.ShapeDtypeStruct((hs, cols), F32),
            jax.ShapeDtypeStruct((hs, quart), F32),
            jax.ShapeDtypeStruct((4 * hs, cols), F32),
            jax.ShapeDtypeStruct((1, 1), F32),
            jax.ShapeDtypeStruct((1, scen), F32),
        ),
        in_specs=[smem, moving, moving, fixed(lines // hs, hs, cols), *smalls],
        out_specs=(moving, fixed(hs, cols), *smalls),
        compiler_params=pltpu.CompilerParams(vmem_limit_bytes=24 * 2**20),
    )(section_three, outs[0], stay(hour_duals.reshape(rows, cols)), *outs[1:])
    return (
        duals_new.reshape(scen, hours, cols),
        first_avg,
        second_avg.reshape(1, hs, quart),
        third_avg.reshape(4, hs, cols),
        level.reshape(1),
        eta_new.reshape(scen),
    )


def solution(mesh):
    both = ("groups", "node")
    cube = P(both, None, None)
    in_specs = (
        cube,
        cube,
        P(),
        P(both),
        P(both),
        P("groups", None),
        cube,
        cube,
        P("groups"),
        P(both),
    )
    out_specs = (cube, P("groups", None), cube, cube, P("groups"), P(both))
    return jax.shard_map(
        functools.partial(body, mesh.shape["node"]),
        mesh=mesh,
        in_specs=in_specs,
        out_specs=out_specs,
        check_vma=False,
    )
```
